256 devices in a mesh: block: 32 (over x_lo, z, core), lane: 8 (over x_hi, y).
Axes of the slice: x: 4 (x_hi: 2, x_lo: 2; x = x_hi * 2 + x_lo), y: 4, z: 8, core: 2. Of those that a mesh axis runs over, the one named last changes fastest.
Arguments:
- images: float32 [16384, 1152], P('block'), may hold values from -1.253025 to 1.253025
- texts: float32 [16384, 1152], P('block'), may hold values from -1.253025 to 1.253025
- labels: int32 [16384], P('block'), may hold values from 0 to 16383, each once
Outputs:
- image_grad: float32 [16384, 1152], P(('block', 'lane'))
- text_grad: float32 [16384, 1152], P(('block', 'lane'))
The draws below stay inside these ranges and needn't reach their ends.
Inputs may be any that keep to these rules, and one draw needn't show every extreme that they name: `labels`: each text row is the partner of exactly one image row.
All inputs are finite; a program needn't handle non-finite values.
Results may differ from the reference program's by a relative error of at most 0.004.
Values may be sent and summed in bfloat16 or wider, within the bound.
No kernel may reach another device: no remote copies, remote signals or barrier semaphores. Data moves between devices by JAX's collectives and lax.ppermute only.
A program may use at most 64 MiB of HBM per device.

```python
import jax
import jax.numpy as jnp
from jax import lax

D = 1152
ROWS_DEV = 512
TOTAL = 16384


def block_levels(key, extent, pieces, least, largest):
    def one(axis_at, parts):
        draws = jax.random.uniform(jax.random.fold_in(jax.random.fold_in(key, 6), axis_at), (parts,), jnp.float32, least / len(pieces), largest / len(pieces))
        return jnp.repeat(jnp.exp(draws), extent[axis_at] // parts).reshape((-1,) + (1,) * (len(extent) - axis_at - 1))

    level = one(*pieces[0])
    for cut in pieces[1:]:
        level = level * one(*cut)
    return level


def normal_values(own_key, shape, scale, bound, pieces=(), held_as=jnp.bfloat16):
    array = jax.random.normal(own_key, shape, jnp.float32) * scale
    if len(pieces) > 0:
        array = block_levels(own_key, shape, pieces, -0.22, 0.18) * array
    return jnp.clip(array, min=-bound, max=bound).astype(held_as)


def setup_inputs(seed: int = 0) -> dict:
    splits = jax.random.split(jax.random.key(seed), 4)
    images = normal_values(splits[0], (TOTAL, D), (1.22 * D ** -0.25), 1.253025, ((0, 32),), jnp.float32)
    texts = normal_values(splits[1], (TOTAL, D), (1.22 * D ** -0.25), 1.253025, ((0, 32),), jnp.float32)
    labels = jax.random.permutation(splits[2], TOTAL).astype(jnp.int32)
    return dict(images=images, texts=texts, labels=labels)


logit_bias = -6.0


def reference(images, texts, labels):
    total = images.shape[0]
    width = images.shape[1]
    count = total // ROWS_DEV
    image_low = lax.optimization_barrier(images.astype(jnp.bfloat16)).astype(jnp.float32)
    text_low = lax.optimization_barrier(texts.astype(jnp.bfloat16)).astype(jnp.float32)
    image_blocks = image_low.reshape(count, ROWS_DEV, width)
    label_blocks = labels.reshape(count, ROWS_DEV)
    columns = jnp.arange(total, dtype=jnp.int32)

    def one_block(text_total, piece):
        image_piece, label_piece = piece
        logits = jnp.dot(image_piece, text_low.T, preferred_element_type=jnp.float32) + logit_bias
        positive = (label_piece[:, None] == columns[None, :]).astype(jnp.float32)
        weights = (jax.nn.sigmoid(logits) - positive).astype(jnp.bfloat16)
        weights = lax.optimization_barrier(weights).astype(jnp.float32)
        image_part = jnp.dot(weights, text_low, preferred_element_type=jnp.float32)
        text_total = text_total + jnp.dot(weights.T, image_piece, preferred_element_type=jnp.float32)
        return text_total, image_part

    text_grad, image_parts = lax.scan(one_block, jnp.zeros((total, width), jnp.float32), (image_blocks, label_blocks))
    return image_parts.reshape(total, width), text_grad
```

```python
import functools

import jax
import jax.numpy as jnp
from jax import lax
from jax.experimental import pallas as pl
from jax.experimental.pallas import tpu as pltpu
from jax.sharding import PartitionSpec as P

logit_bias = -6.0
XL, Z, C, XH, Y = 2, 8, 2, 2, 4
X = XL * XH
AXES = ("block", "lane")
low = jnp.bfloat16
MIB = 1 << 20


def flat(x, y, z, c):
    return (((x % 2) * Z + z) * C + c) * (XH * Y) + (x // 2) * Y + y


def send(value, dx=0, dy=0, dz=0, dc=0):
    pairs = []
    for x in range(X):
        for y in range(Y):
            for z in range(Z):
                for c in range(C):
                    to = flat((x + dx) % X, (y + dy) % Y, (z + dz) % Z, (c + dc) % C)
                    pairs.append((flat(x, y, z, c), to))
    return lax.ppermute(value, AXES, pairs)


def prep_kernel(index_ref, images_ref, own_ref, far_ref, held, sems):
    copies = []
    for i in range(8):
        start = pl.multiple_of(index_ref[i] * 64, 64)
        copy = pltpu.make_async_copy(images_ref.at[pl.ds(start, 64)], held.at[i], sems.at[i])
        copy.start()
        copies.append(copy)
    for i in range(8):
        copies[i].wait()
        out = own_ref if i < 4 else far_ref
        dy = i % 4
        out[pl.ds(dy * 32, 32), :] = held[i, :32, :].astype(low)
        out[pl.ds(128 + dy * 32, 32), :] = held[i, 32:, :].astype(low)


def prep(images, index):
    width = images.shape[1]
    shape = jax.ShapeDtypeStruct((256, width), low)
    return pl.pallas_call(
        prep_kernel,
        out_shape=(shape, shape),
        in_specs=[pl.BlockSpec(memory_space=pltpu.SMEM), pl.BlockSpec(memory_space=pl.ANY)],
        out_specs=(pl.BlockSpec(memory_space=pltpu.VMEM),) * 2,
        scratch_shapes=[pltpu.VMEM((8, 64, width), jnp.float32), pltpu.SemaphoreType.DMA((8,))],
        compiler_params=pltpu.CompilerParams(vmem_limit_bytes=8 * MIB),
        cost_estimate=pl.CostEstimate(flops=0, bytes_accessed=4 << 20, transcendentals=0),
    )(index, images)


def tile_kernel(pieces, first, last, *refs):
    refs = list(refs)
    images = [refs.pop(0) for _ in range(4)]
    labels = refs.pop(0)
    columns = refs.pop(0)
    texts = [refs.pop(0) for _ in range(2 * pieces)]
    held = None if first else refs.pop(0)
    if last:
        x_out = [refs.pop(0) for _ in range(4)]
        y_out = [refs.pop(0) for _ in range(4)]
    else:
        sums_ref = refs.pop(0)
    own_out = refs.pop(0)
    other_out = refs.pop(0)
    text_scratch, text_sum = refs
    half = 64 * pieces
    for i in range(2 * pieces):
        text_scratch[pl.ds(i * 64, 64), :] = texts[i][...]
    text = text_scratch[...]
    for a in range(4):
        image = images[a][...]
        logits = (
            lax.dot_general(image, text, (((1,), (1,)), ((), ())), preferred_element_type=jnp.float32)
            + logit_bias
        )
        positive = (labels[pl.ds(a * 256, 256), :] == columns[...]).astype(jnp.float32)
        weights = (jax.nn.sigmoid(logits) - positive).astype(low)
        term = lax.dot_general(
            weights, image, (((0,), (0,)), ((), ())), preferred_element_type=jnp.float32
        )
        if a == 0:
            text_sum[...] = term
        else:
            text_sum[...] += term
        total = jnp.dot(weights, text, preferred_element_type=jnp.float32)
        if not first:
            total = total + held[pl.ds(a * 256, 256), :]
        if last:
            total = total.astype(low)
            x_out[a][...] = total[:128]
            for dy in range(4):
                y_out[dy][pl.ds(a * 32, 32), :] = total[128 + dy * 32 : 160 + dy * 32]
        else:
            sums_ref[pl.ds(a * 256, 256), :] = total
    own_out[...] = text_sum[:half, :].astype(own_out.dtype)
    other_out[...] = text_sum[half:, :].astype(low)


def tile(images, labels, columns, own_texts, other_texts, held, last):
    pieces = len(own_texts)
    first = held is None
    width = images[0].shape[1]
    half = 64 * pieces
    vmem = pl.BlockSpec(memory_space=pltpu.VMEM)
    outs = []
    if last:
        outs += [jax.ShapeDtypeStruct((128, width), low)] * 8
    else:
        outs += [jax.ShapeDtypeStruct((1024, width), jnp.float32)]
    outs += [jax.ShapeDtypeStruct((half, width), jnp.float32), jax.ShapeDtypeStruct((half, width), low)]
    args = [*images, labels, columns, *own_texts, *other_texts]
    if not first:
        args.append(held)
    return pl.pallas_call(
        functools.partial(tile_kernel, pieces, first, last),
        out_shape=tuple(outs),
        in_specs=[vmem] * len(args),
        out_specs=(vmem,) * len(outs),
        scratch_shapes=[
            pltpu.VMEM((2 * half, width), low),
            pltpu.VMEM((2 * half, width), jnp.float32),
        ],
        compiler_params=pltpu.CompilerParams(vmem_limit_bytes=32 * MIB),
        cost_estimate=pl.CostEstimate(
            flops=6 * 1024 * 2 * half * width, bytes_accessed=8 << 20, transcendentals=1024 * 2 * half
        ),
    )(*args)


def on_device(images, texts, labels):
    width = images.shape[1]
    block = lax.axis_index("block")
    lane = lax.axis_index("lane")
    xl, z, c = block // 16, block // 2 % 8, block % 2
    xh, y = lane // 4, lane % 4

    text_own = lax.dynamic_slice_in_dim(texts, lane * 64, 64, 0).astype(low)
    text_z = {0: text_own}
    for d in (4, 3, 5, 2, 6, 1, 7):
        text_z[d] = send(text_own, dz=-d)

    index = jnp.stack([(xh ^ a) * 4 + (y + b) % 4 for a in range(2) for b in range(4)])
    own, far = prep(images, index)
    near_right = send(own, dx=-1)
    near_left = send(own, dx=1)
    image_parts = [own, near_right, far, near_left]

    order = labels.reshape(2, 4, 2, 32)
    order = jnp.where(xh == 1, order[::-1], order)
    doubled = jnp.concatenate([order, order], axis=1)
    order = lax.dynamic_slice_in_dim(doubled, y, 4, 1).transpose(0, 2, 1, 3).reshape(2, 256)
    label_rows = jnp.concatenate([order[0], send(order[0], dx=-1), order[1], send(order[0], dx=1)])
    label_rows = label_rows.reshape(1024, 1)

    def column_ids(group):
        ids = []
        for core in (c, 1 - c):
            for d in group:
                start = ((xl * Z + (z + d) % Z) * C + core) * 512 + lane * 64
                ids.append(start + jnp.arange(64, dtype=jnp.int32))
        return jnp.concatenate(ids)[None, :]

    groups = ((0, 1, 7, 2), (6, 3, 5, 4))
    held = None
    text_terms = {}
    for i, group in enumerate(groups):
        last = i == len(groups) - 1
        own_texts = [text_z[d] for d in group]
        other_texts = [send(text_z[d], dc=1) for d in group]
        outs = tile(image_parts, label_rows, column_ids(group), own_texts, other_texts, held, last)
        if last:
            x_parts, y_parts = outs[:4], outs[4:8]
        else:
            held = outs[0]
        mine, theirs = outs[-2:]
        both = mine + send(theirs, dc=1).astype(jnp.float32)
        for j, d in enumerate(group):
            term = both[j * 64 : j * 64 + 64]
            text_terms[d] = term if d == 0 else send(term.astype(low), dz=d).astype(jnp.float32)

    x_sum = x_parts[0].astype(jnp.float32)
    y_sum = y_parts[0].astype(jnp.float32)
    for d in (2, 1, 3):
        x_sum = x_sum + send(x_parts[d], dx=d).astype(jnp.float32)
        y_sum = y_sum + send(y_parts[d], dy=d).astype(jnp.float32)
    upper = x_sum[:32]
    lower = y_sum[:32]
    for d in (2, 1, 3):
        upper = upper + send(x_sum[d * 32 : d * 32 + 32].astype(low), dy=d).astype(jnp.float32)
        lower = lower + send(y_sum[d * 32 : d * 32 + 32].astype(low), dx=d).astype(jnp.float32)
    image_out = jnp.concatenate([upper, lower], axis=0)
    text_out = text_terms[0]
    for d in range(1, Z):
        text_out = text_out + text_terms[d]
    return image_out, text_out


def solution(mesh):
    placed = (P("block", None), P("block", None), P("block"))
    return jax.shard_map(
        on_device,
        mesh=mesh,
        in_specs=placed,
        out_specs=(P(("block", "lane"), None), P(("block", "lane"), None)),
        check_vma=False,
    )
```

```python
import functools

import jax
import jax.numpy as jnp
from jax import lax
from jax.experimental import pallas as pl
from jax.experimental.pallas import tpu as pltpu
from jax.sharding import PartitionSpec as P

logit_bias = -6.0
Z, C, X, Y = 8, 2, 4, 4
AXES = ("block", "lane")
ROWS = 512
SHARE = 64
low = jnp.bfloat16
f32 = jnp.float32
MIB = 1 << 20
VMEM = pl.BlockSpec(memory_space=pltpu.VMEM)
ANY = pl.BlockSpec(memory_space=pl.ANY)


def flat(x, y, z, c):
    return (((x % 2) * Z + z) * C + c) * (X // 2 * Y) + (x // 2) * Y + y


def send(value, step):
    pairs = []
    for x in range(X):
        for y in range(Y):
            for z in range(Z):
                for c in range(C):
                    dx, dy, dz, dc = step(c)
                    to = flat((x + dx) % X, (y + dy) % Y, (z + dz) % Z, (c + dc) % C)
                    pairs.append((flat(x, y, z, c), to))
    return lax.ppermute(value, AXES, pairs)


def to_core(value):
    return send(value, lambda c: (0, 0, 0, 1))


def to_x(value, d):
    return send(value, lambda c: (d, 0, 0, 0))


def to_z(value, d):
    return send(value, lambda c: (0, 0, -d if c else d, 0))


def first_stage(value, d):
    return send(value, lambda c: (0, d, 0, 0) if c else (d, 0, 0, 0))


def second_stage(value, d):
    return send(value, lambda c: (d, 0, 0, 0) if c else (0, d, 0, 0))


def place():
    block = lax.axis_index("block")
    lane = lax.axis_index("lane")
    return block // 16, block // 2 % 8, block % 2, lane // 4, lane % 4


def prep_kernel(far, where_ref, images_ref, texts_ref, labels_ref, *refs):
    refs = list(refs)
    text_out = None if far else refs.pop(0)
    image_out, held, text_held, sems = refs
    xh, y = where_ref[3], where_ref[4]
    if not far:
        start = pl.multiple_of((xh * Y + y) * SHARE, SHARE)
        text_copy = pltpu.make_async_copy(texts_ref.at[pl.ds(start, SHARE)], text_held, sems.at[4])
        text_copy.start()
    half = 1 - xh if far else xh
    copies = []
    for i in range(Y):
        row = pl.multiple_of((half * Y + lax.rem(y + i, Y)) * SHARE, SHARE)
        copy = pltpu.make_async_copy(images_ref.at[pl.ds(row, SHARE)], held.at[i], sems.at[i])
        copy.start()
        copies.append(copy)
    labels = jnp.concatenate([labels_ref[pl.ds(2 * half, 1), :], labels_ref[pl.ds(2 * half + 1, 1), :]], axis=1)
    labels = jnp.broadcast_to(labels, (16, 256))
    labels = pltpu.roll(labels, lax.rem(Y - y, Y) * SHARE, 1)
    row = lax.broadcasted_iota(jnp.int32, (16, 256), 0)
    digits = jnp.where(row == 0, labels >> 7, jnp.where(row == 1, labels & 127, 0))
    image_out[256:272, :256] = digits.astype(f32).astype(low)
    image_out[256:272, 256:] = jnp.zeros((16, image_out.shape[1] - 256), low)
    if not far:
        text_copy.wait()
        text_out[...] = text_held[...].astype(low)
    for i in range(Y):
        copies[i].wait()
        image_out[i * SHARE : (i + 1) * SHARE, :] = held[i].astype(low)


def prep(where, images, texts, labels, far):
    width = images.shape[1]
    outs = [] if far else [jax.ShapeDtypeStruct((SHARE, width), low)]
    outs.append(jax.ShapeDtypeStruct((272, width), low))
    return pl.pallas_call(
        functools.partial(prep_kernel, far),
        out_shape=tuple(outs),
        in_specs=[pl.BlockSpec(memory_space=pltpu.SMEM), ANY, ANY, VMEM],
        out_specs=(VMEM,) * len(outs),
        scratch_shapes=[
            pltpu.VMEM((Y, SHARE, width), f32),
            pltpu.VMEM((SHARE, width), f32),
            pltpu.SemaphoreType.DMA((5,)),
        ],
        compiler_params=pltpu.CompilerParams(vmem_limit_bytes=58 * MIB),
        cost_estimate=pl.CostEstimate(flops=0, bytes_accessed=3 << 20, transcendentals=0),
    )(where, images, texts, labels)


def tile_kernel(group, first, last, where_ref, *refs):
    refs = list(refs)
    if first:
        parts = [refs.pop(0) for _ in range(4)]
    else:
        images_ref = refs.pop(0)
        labels_ref = refs.pop(0)
        held = refs.pop(0)
    texts = [(refs.pop(0), refs.pop(0)) for _ in group]
    if first:
        images_ref = refs.pop(0)
        labels_ref = refs.pop(0)
    if last:
        image_outs = [refs.pop(0) for _ in range(4)]
    else:
        sums_ref = refs.pop(0)
    keep_ref = refs.pop(0)
    give_ref = refs.pop(0)
    text_ref, weight_ref = refs
    n = text_ref.shape[0]
    half = n // 2
    xl, z, c, xh, y = (where_ref[i] for i in range(5))
    if first:
        for a in range(4):
            images_ref[a * 256 : (a + 1) * 256, :] = parts[a][:256, :]
            digits = parts[a][256:272, :256].astype(f32)
            both = digits[0:1] * 128.0 + digits[1:2]
            labels_ref[:, a * 256 : (a + 1) * 256] = jnp.broadcast_to(both, (8, 256))
    numbers = [[], []]
    at = 0
    sign = 1 - 2 * c
    for d, pair in zip(group, texts):
        rows = pair[0].shape[0]
        for side in range(2):
            offset = at + side * half
            text_ref[offset : offset + rows, :] = pair[side][...]
            if d in (0, 4):
                cores = (c,) if side == 0 else (1 - c,)
                chip = lax.rem(z + d, Z)
            else:
                cores = (c, 1 - c) if side == 0 else (1 - c, c)
                chip = lax.rem(z + Z + sign * (d if side == 0 else -d), Z)
            for core in cores:
                start = ((xl * Z + chip) * C + core) * ROWS + (xh * Y + y) * SHARE
                numbers[side].append(lax.broadcasted_iota(jnp.int32, (SHARE, 1), 0) + start)
        at += rows
    numbers = jnp.concatenate(numbers[0] + numbers[1], axis=0).astype(f32)
    text = text_ref[...]
    for a in range(4):
        cut = slice(a * 256, (a + 1) * 256)
        logits = (
            lax.dot_general(text, images_ref[cut, :], (((1,), (1,)), ((), ())), preferred_element_type=f32)
            + logit_bias
        )
        positive = (labels_ref[0:1, cut] == numbers).astype(f32)
        weight_ref[:, cut] = (jax.nn.sigmoid(logits) - positive).astype(low)
    text_term = jnp.dot(weight_ref[...], images_ref[...], preferred_element_type=f32)
    keep_ref[...] = text_term[:half]
    give_ref[...] = text_term[half:].astype(low)
    total = lax.dot_general(weight_ref[...], text, (((0,), (0,)), ((), ())), preferred_element_type=f32)
    if not first:
        total = total + held[...]
    if last:
        total = total.astype(low)

        @pl.when(c == 0)
        def _():
            for a in range(4):
                image_outs[a][...] = total[a * 256 : (a + 1) * 256]

        @pl.when(c == 1)
        def _():
            for a in range(4):
                for b in range(4):
                    start = a * 256 + b * SHARE
                    image_outs[b][a * SHARE : (a + 1) * SHARE, :] = total[start : start + SHARE]
    else:
        sums_ref[...] = total


def tile(where, state, group, texts, last):
    first = len(state) == 4
    width = state[0].shape[1]
    half = sum(pair[0].shape[0] for pair in texts)
    n = 2 * half
    outs = []
    if first:
        outs.append(jax.ShapeDtypeStruct((1024, width), low))
        outs.append(jax.ShapeDtypeStruct((8, 1024), f32))
    if last:
        outs += [jax.ShapeDtypeStruct((256, width), low)] * 4
    else:
        outs.append(jax.ShapeDtypeStruct((1024, width), f32))
    outs += [jax.ShapeDtypeStruct((half, width), f32), jax.ShapeDtypeStruct((half, width), low)]
    args = [where, *state]
    for pair in texts:
        args += pair
    results = pl.pallas_call(
        functools.partial(tile_kernel, group, first, last),
        out_shape=tuple(outs),
        in_specs=[pl.BlockSpec(memory_space=pltpu.SMEM)] + [VMEM] * (len(args) - 1),
        out_specs=(VMEM,) * len(outs),
        scratch_shapes=[pltpu.VMEM((n, width), low), pltpu.VMEM((n, 1024), low)],
        compiler_params=pltpu.CompilerParams(vmem_limit_bytes=28 * MIB),
        cost_estimate=pl.CostEstimate(
            flops=6 * 1024 * n * width, bytes_accessed=4 << 20, transcendentals=1024 * n
        ),
    )(*args)
    keep, give = results[-2:]
    if first:
        state = results[:3]
    elif last:
        state = results[:4]
    else:
        state = (state[0], state[1], results[0])
    return state, keep, give


def on_device(images, texts, labels):
    where = jnp.stack(place()).astype(jnp.int32)
    label_rows = labels.reshape(4, 128)
    text_own, image_near = prep(where, images, texts, label_rows, False)
    text_other = to_core(text_own)
    image_right = to_x(image_near, -1)
    image_left = to_x(image_near, 1)
    chunk = jnp.concatenate([text_own, text_other], axis=0)
    arrived = {}
    for d in (3, 2, 1):
        arrived[d] = to_z(chunk, -d)
    arrived[4] = to_z(text_own, 4)
    (image_far,) = prep(where, images, texts, label_rows, True)
    state = (image_near, image_right, image_far, image_left)

    groups = ((0, 1), (2,), (3, 4))
    parts = {}
    for i, group in enumerate(groups):
        pairs = [(text_own, text_other) if d == 0 else (arrived[d], to_core(arrived[d])) for d in group]
        state, keep, give = tile(where, state, group, pairs, i == len(groups) - 1)
        at = 0
        if group[0] == 0:
            own_keep, own_give = keep[:SHARE], give[:SHARE]
            keep, give = keep[SHARE:], give[SHARE:]
            group = group[1:]
        both = (keep + to_core(give).astype(f32)).astype(low)
        for d in group:
            rows = SHARE if d == 4 else 2 * SHARE
            parts[d] = to_z(both[at : at + rows], d).astype(f32)
            at += rows

    image_sum = state[0].astype(f32)
    for d in (2, 1, 3):
        image_sum = image_sum + first_stage(state[d], d).astype(f32)
    image_out = image_sum[:SHARE]
    for d in (2, 1, 3):
        piece = image_sum[d * SHARE : (d + 1) * SHARE].astype(low)
        image_out = image_out + second_stage(piece, d).astype(f32)

    text_sum = parts[1] + parts[2] + parts[3]
    give = (text_sum[SHARE:] + own_give.astype(f32)).astype(low)
    text_out = text_sum[:SHARE] + own_keep + parts[4] + to_core(give).astype(f32)
    return image_out, text_out


def solution(mesh):
    placed = (P("block", None), P("block", None), P("block"))
    return jax.shard_map(
        on_device,
        mesh=mesh,
        in_specs=placed,
        out_specs=(P(("block", "lane"), None), P(("block", "lane"), None)),
        check_vma=False,
    )
```

```python
import functools

import jax
import jax.numpy as jnp
from jax import lax
from jax.experimental import pallas as pl
from jax.experimental.pallas import tpu as pltpu
from jax.sharding import PartitionSpec as P

logit_bias = -6.0
Z, C, X, Y = 8, 2, 4, 4
AXES = ("block", "lane")
ROWS = 512
SHARE = 64
low = jnp.bfloat16
f32 = jnp.float32
MIB = 1 << 20
VMEM = pl.BlockSpec(memory_space=pltpu.VMEM)
HBM = pl.BlockSpec(memory_space=pltpu.HBM)


def flat(x, y, z, c):
    return (((x % 2) * Z + z) * C + c) * (X // 2 * Y) + (x // 2) * Y + y


def send(value, step):
    pairs = []
    for x in range(X):
        for y in range(Y):
            for z in range(Z):
                for c in range(C):
                    dx, dy, dz, dc = step(c)
                    to = flat((x + dx) % X, (y + dy) % Y, (z + dz) % Z, (c + dc) % C)
                    pairs.append((flat(x, y, z, c), to))
    return lax.ppermute(value, AXES, pairs)


def to_core(value):
    return send(value, lambda c: (0, 0, 0, 1))


def to_x(value, d):
    return send(value, lambda c: (d, 0, 0, 0))


def to_z(value, d):
    return send(value, lambda c: (0, 0, -d if c else d, 0))


def first_stage(value, d):
    return send(value, lambda c: (0, d, 0, 0) if c else (d, 0, 0, 0))


def second_stage(value, d):
    return send(value, lambda c: (d, 0, 0, 0) if c else (0, d, 0, 0))


def place():
    block = lax.axis_index("block")
    lane = lax.axis_index("lane")
    return block // 16, block // 2 % 8, block % 2, lane // 4, lane % 4


def prep_kernel(far, where_ref, images_ref, texts_ref, labels_ref, *refs):
    refs = list(refs)
    text_out = None if far else refs.pop(0)
    image_out, held, text_held, sems = refs
    xh, y = where_ref[3], where_ref[4]
    if not far:
        start = pl.multiple_of((xh * Y + y) * SHARE, SHARE)
        text_copy = pltpu.make_async_copy(texts_ref.at[pl.ds(start, SHARE)], text_held, sems.at[4])
        text_copy.start()
    half = 1 - xh if far else xh
    copies = []
    for i in range(Y):
        row = pl.multiple_of((half * Y + lax.rem(y + i, Y)) * SHARE, SHARE)
        copy = pltpu.make_async_copy(images_ref.at[pl.ds(row, SHARE)], held.at[i], sems.at[i])
        copy.start()
        copies.append(copy)
    labels = jnp.concatenate([labels_ref[pl.ds(2 * half, 1), :], labels_ref[pl.ds(2 * half + 1, 1), :]], axis=1)
    labels = jnp.broadcast_to(labels, (16, 256))
    labels = pltpu.roll(labels, lax.rem(Y - y, Y) * SHARE, 1)
    row = lax.broadcasted_iota(jnp.int32, (16, 256), 0)
    digits = jnp.where(row == 0, labels >> 7, jnp.where(row == 1, labels & 127, 0))
    image_out[256:272, :256] = digits.astype(f32).astype(low)
    image_out[256:272, 256:] = jnp.zeros((16, image_out.shape[1] - 256), low)
    if not far:
        text_copy.wait()
        text_out[...] = text_held[...].astype(low)
    for i in range(Y):
        copies[i].wait()
        image_out[i * SHARE : (i + 1) * SHARE, :] = held[i].astype(low)


def prep(where, images, texts, labels, far):
    width = images.shape[1]
    outs = [] if far else [jax.ShapeDtypeStruct((SHARE, width), low)]
    outs.append(jax.ShapeDtypeStruct((272, width), low))
    return pl.pallas_call(
        functools.partial(prep_kernel, far),
        out_shape=tuple(outs),
        in_specs=[pl.BlockSpec(memory_space=pltpu.SMEM), HBM, HBM, VMEM],
        out_specs=(VMEM,) * len(outs),
        scratch_shapes=[
            pltpu.VMEM((Y, SHARE, width), f32),
            pltpu.VMEM((SHARE, width), f32),
            pltpu.SemaphoreType.DMA((5,)),
        ],
        compiler_params=pltpu.CompilerParams(vmem_limit_bytes=52 * MIB),
        cost_estimate=pl.CostEstimate(flops=0, bytes_accessed=3 << 20, transcendentals=0),
    )(where, images, texts, labels)


def tile_kernel(group, gives, first, last, where_ref, *refs):
    refs = list(refs)
    if first:
        parts = [refs.pop(0) for _ in range(4)]
    else:
        images_ref = refs.pop(0)
        labels_ref = refs.pop(0)
        held = refs.pop(0)
    texts = [(refs.pop(0), refs.pop(0)) for _ in group]
    if first:
        images_ref = refs.pop(0)
        labels_ref = refs.pop(0)
    if last:
        image_outs = [refs.pop(0) for _ in range(4)]
    else:
        sums_ref = refs.pop(0)
    keep_refs = [refs.pop(0) for _ in group]
    give_refs = [refs.pop(0) for _ in range(gives)]
    text_ref, weight_ref = refs
    n = text_ref.shape[0]
    half = n // 2
    xl, z, c, xh, y = (where_ref[i] for i in range(5))
    if first:
        for a in range(4):
            images_ref[a * 256 : (a + 1) * 256, :] = parts[a][:256, :]
            digits = parts[a][256:272, :256].astype(f32)
            both = digits[0:1] * 128.0 + digits[1:2]
            labels_ref[:, a * 256 : (a + 1) * 256] = jnp.broadcast_to(both, (8, 256))
    numbers = [[], []]
    at = 0
    sign = 1 - 2 * c
    for d, pair in zip(group, texts):
        rows = pair[0].shape[0]
        for side in range(2):
            offset = at + side * half
            text_ref[offset : offset + rows, :] = pair[side][...]
            if d in (0, 4):
                cores = (c,) if side == 0 else (1 - c,)
                chip = lax.rem(z + d, Z)
            else:
                cores = (c, 1 - c) if side == 0 else (1 - c, c)
                chip = lax.rem(z + Z + sign * (d if side == 0 else -d), Z)
            for core in cores:
                start = ((xl * Z + chip) * C + core) * ROWS + (xh * Y + y) * SHARE
                numbers[side].append(lax.broadcasted_iota(jnp.int32, (SHARE, 1), 0) + start)
        at += rows
    numbers = jnp.concatenate(numbers[0] + numbers[1], axis=0).astype(f32)
    text = text_ref[...]
    for a in range(4):
        cut = slice(a * 256, (a + 1) * 256)
        logits = (
            lax.dot_general(text, images_ref[cut, :], (((1,), (1,)), ((), ())), preferred_element_type=f32)
            + logit_bias
        )
        positive = (labels_ref[0:1, cut] == numbers).astype(f32)
        weight_ref[:, cut] = (jax.nn.sigmoid(logits) - positive).astype(low)
    text_term = jnp.dot(weight_ref[...], images_ref[...], preferred_element_type=f32)
    at = 0
    for ref in keep_refs:
        ref[...] = text_term[at : at + ref.shape[0]]
        at += ref.shape[0]
    for ref in give_refs:
        ref[...] = text_term[at : at + ref.shape[0]].astype(low)
        at += ref.shape[0]
    total = lax.dot_general(weight_ref[...], text, (((0,), (0,)), ((), ())), preferred_element_type=f32)
    if not first:
        total = total + held[...]
    if last:
        total = total.astype(low)

        @pl.when(c == 0)
        def _():
            for a in range(4):
                image_outs[a][...] = total[a * 256 : (a + 1) * 256]

        @pl.when(c == 1)
        def _():
            for a in range(4):
                for b in range(4):
                    start = a * 256 + b * SHARE
                    image_outs[b][a * SHARE : (a + 1) * SHARE, :] = total[start : start + SHARE]
    else:
        sums_ref[...] = total


def tile(where, state, group, texts, last):
    first = len(state) == 4
    width = state[0].shape[1]
    half = sum(pair[0].shape[0] for pair in texts)
    n = 2 * half
    outs = []
    if first:
        outs.append(jax.ShapeDtypeStruct((1024, width), low))
        outs.append(jax.ShapeDtypeStruct((8, 1024), f32))
    if last:
        outs += [jax.ShapeDtypeStruct((256, width), low)] * 4
    else:
        outs.append(jax.ShapeDtypeStruct((1024, width), f32))
    sizes = [pair[0].shape[0] for pair in texts]
    give_sizes = sizes if first else [half]
    outs += [jax.ShapeDtypeStruct((size, width), f32) for size in sizes]
    outs += [jax.ShapeDtypeStruct((size, width), low) for size in give_sizes]
    args = [where, *state]
    for pair in texts:
        args += pair
    results = pl.pallas_call(
        functools.partial(tile_kernel, group, len(give_sizes), first, last),
        out_shape=tuple(outs),
        in_specs=[pl.BlockSpec(memory_space=pltpu.SMEM)] + [VMEM] * (len(args) - 1),
        out_specs=(VMEM,) * len(outs),
        scratch_shapes=[pltpu.VMEM((n, width), low), pltpu.VMEM((n, 1024), low)],
        compiler_params=pltpu.CompilerParams(vmem_limit_bytes=28 * MIB),
        cost_estimate=pl.CostEstimate(
            flops=6 * 1024 * n * width, bytes_accessed=4 << 20, transcendentals=1024 * n
        ),
    )(*args)
    cut = len(results) - len(give_sizes)
    keep, give = results[cut - len(sizes) : cut], results[cut:]
    if first:
        state = results[:3]
    elif last:
        state = results[:4]
    else:
        state = (state[0], state[1], results[0])
    return state, keep, give


def on_device(images, texts, labels):
    where = jnp.stack(place()).astype(jnp.int32)
    label_rows = labels.reshape(4, 128)
    text_own, image_near = prep(where, images, texts, label_rows, False)
    text_other = to_core(text_own)
    image_right = to_x(image_near, -1)
    image_left = to_x(image_near, 1)
    chunk = jnp.concatenate([text_own, text_other], axis=0)
    arrived = {2: to_z(chunk, -2), 1: to_z(chunk, -1)}
    swapped_1 = to_core(arrived[1])
    arrived[2], swapped_1 = lax.optimization_barrier((arrived[2], swapped_1))
    arrived[3] = to_z(arrived[2], -1)
    arrived[4] = to_z(arrived[2][:SHARE], -2)
    (image_far,) = prep(where, images, texts, label_rows, True)
    image_right, _ = lax.optimization_barrier((image_right, arrived[2]))
    state = (image_near, image_right, image_far, image_left)

    pairs = [(text_own, text_other), (arrived[1], swapped_1)]
    state, keep, give = tile(where, state, (0, 1), pairs, False)
    own_keep, own_give = keep[0], give[0]
    term_1 = (keep[1] + to_core(give[1]).astype(f32)).astype(low)

    pairs = [(arrived[2], to_core(arrived[2]))]
    state, keep, give = tile(where, state, (2,), pairs, False)
    term_2 = keep[0] + to_core(give[0]).astype(f32)

    pairs = [(arrived[d], to_core(arrived[d])) for d in (3, 4)]
    held, term_1 = lax.optimization_barrier((state[2], term_1))
    state, keep, give = tile(where, (state[0], state[1], held), (3, 4), pairs, True)
    swapped = to_core(give[0]).astype(f32)
    from_3 = to_z((keep[0] + swapped[: 2 * SHARE]).astype(low), 1).astype(f32)
    from_4 = to_z((keep[1] + swapped[2 * SHARE :]).astype(low), 2).astype(f32)
    upper = term_2[:SHARE] + from_3[:SHARE] + from_4
    lower = term_2[SHARE:] + from_3[SHARE:]
    term_2 = jnp.concatenate([upper, lower], axis=0).astype(low)
    parts = to_z(term_1, 1).astype(f32) + to_z(term_2, 2).astype(f32)

    image_sum = state[0].astype(f32)
    for d in (2, 1, 3):
        image_sum = image_sum + first_stage(state[d], d).astype(f32)
    image_out = image_sum[:SHARE]
    for d in (2, 1, 3):
        piece = image_sum[d * SHARE : (d + 1) * SHARE].astype(low)
        image_out = image_out + second_stage(piece, d).astype(f32)

    give = (parts[SHARE:] + own_give.astype(f32)).astype(low)
    text_out = parts[:SHARE] + own_keep + to_core(give).astype(f32)
    return image_out, text_out


def solution(mesh):
    placed = (P("block", None), P("block", None), P("block"))
    return jax.shard_map(
        on_device,
        mesh=mesh,
        in_specs=placed,
        out_specs=(P(("block", "lane"), None), P(("block", "lane"), None)),
        check_vma=False,
    )
```

```python
import functools

import jax
import jax.numpy as jnp
from jax import lax
from jax.experimental import pallas as pl
from jax.experimental.pallas import tpu as pltpu
from jax.sharding import PartitionSpec as P

logit_bias = -6.0
Z, C, X, Y = 8, 2, 4, 4
AXES = ("block", "lane")
ROWS = 512
SHARE = 64
low = jnp.bfloat16
f32 = jnp.float32
MIB = 1 << 20
ORDER = (2, 1, 3, 0)
VMEM = pl.BlockSpec(memory_space=pltpu.VMEM)
HBM = pl.BlockSpec(memory_space=pltpu.HBM)


def flat(x, y, z, c):
    return (((x % 2) * Z + z) * C + c) * (X // 2 * Y) + (x // 2) * Y + y


def send(value, step):
    pairs = []
    for x in range(X):
        for y in range(Y):
            for z in range(Z):
                for c in range(C):
                    dx, dy, dz, dc = step(c)
                    to = flat((x + dx) % X, (y + dy) % Y, (z + dz) % Z, (c + dc) % C)
                    pairs.append((flat(x, y, z, c), to))
    return lax.ppermute(value, AXES, pairs)


def to_core(value):
    return send(value, lambda c: (0, 0, 0, 1))


def to_x(value, d):
    return send(value, lambda c: (d, 0, 0, 0))


def to_z(value, d):
    return send(value, lambda c: (0, 0, -d if c else d, 0))


def first_stage(value, d):
    return send(value, lambda c: (0, d, 0, 0) if c else (d, 0, 0, 0))


def second_stage(value, d):
    return send(value, lambda c: (d, 0, 0, 0) if c else (0, d, 0, 0))


def place():
    block = lax.axis_index("block")
    lane = lax.axis_index("lane")
    return block // 16, block // 2 % 8, block % 2, lane // 4, lane % 4


def prep_kernel(far, where_ref, images_ref, labels_ref, image_out, held, sems):
    xh, y = where_ref[3], where_ref[4]
    half = 1 - xh if far else xh
    copies = []
    for i in range(Y):
        row = pl.multiple_of((half * Y + lax.rem(y + i, Y)) * SHARE, SHARE)
        copy = pltpu.make_async_copy(images_ref.at[pl.ds(row, SHARE)], held.at[i], sems.at[i])
        copy.start()
        copies.append(copy)
    labels = jnp.concatenate([labels_ref[pl.ds(2 * half, 1), :], labels_ref[pl.ds(2 * half + 1, 1), :]], axis=1)
    labels = jnp.broadcast_to(labels, (16, 256))
    labels = pltpu.roll(labels, lax.rem(Y - y, Y) * SHARE, 1)
    row = lax.broadcasted_iota(jnp.int32, (16, 256), 0)
    digits = jnp.where(row == 0, labels >> 7, jnp.where(row == 1, labels & 127, 0))
    image_out[256:272, :256] = digits.astype(f32).astype(low)
    image_out[256:272, 256:] = jnp.zeros((16, image_out.shape[1] - 256), low)
    for i in range(Y):
        copies[i].wait()
        image_out[i * SHARE : (i + 1) * SHARE, :] = held[i].astype(low)


def prep(where, images, labels, far):
    width = images.shape[1]
    return pl.pallas_call(
        functools.partial(prep_kernel, far),
        out_shape=jax.ShapeDtypeStruct((272, width), low),
        in_specs=[pl.BlockSpec(memory_space=pltpu.SMEM), HBM, VMEM],
        out_specs=VMEM,
        scratch_shapes=[pltpu.VMEM((Y, SHARE, width), f32), pltpu.SemaphoreType.DMA((Y,))],
        compiler_params=pltpu.CompilerParams(vmem_limit_bytes=52 * MIB),
        cost_estimate=pl.CostEstimate(flops=0, bytes_accessed=3 << 20, transcendentals=0),
    )(where, images, labels)


def text_kernel(where_ref, texts_ref, text_out, held, sem):
    row = pl.multiple_of((where_ref[3] * Y + where_ref[4]) * SHARE, SHARE)
    copy = pltpu.make_async_copy(texts_ref.at[pl.ds(row, SHARE)], held, sem)
    copy.start()
    copy.wait()
    text_out[...] = held[...].astype(low)


def own_text(where, texts):
    width = texts.shape[1]
    return pl.pallas_call(
        text_kernel,
        out_shape=jax.ShapeDtypeStruct((SHARE, width), low),
        in_specs=[pl.BlockSpec(memory_space=pltpu.SMEM), HBM],
        out_specs=VMEM,
        scratch_shapes=[pltpu.VMEM((SHARE, width), f32), pltpu.SemaphoreType.DMA],
        compiler_params=pltpu.CompilerParams(vmem_limit_bytes=52 * MIB),
        cost_estimate=pl.CostEstimate(flops=0, bytes_accessed=1 << 19, transcendentals=0),
    )(where, texts)


def arrange(where_ref, parts, images_ref, labels_ref):
    labels = []
    for part in parts:
        digits = part[256:272, :256].astype(f32)
        labels.append(digits[0:1] * 128.0 + digits[1:2])
    core = where_ref[2]

    @pl.when(core == 0)
    def _():
        for k, d in enumerate(ORDER):
            images_ref[k * 256 : (k + 1) * 256, :] = parts[d][:256, :]
            labels_ref[:, k * 256 : (k + 1) * 256] = jnp.broadcast_to(labels[d], (8, 256))

    @pl.when(core == 1)
    def _():
        for k, d in enumerate(ORDER):
            cut = slice(d * SHARE, (d + 1) * SHARE)
            for a in range(4):
                start = k * 256 + a * SHARE
                images_ref[start : start + SHARE, :] = parts[a][cut, :]
            row = jnp.concatenate([labels[a][:, cut] for a in range(4)], axis=1)
            labels_ref[:, k * 256 : (k + 1) * 256] = jnp.broadcast_to(row, (8, 256))


def text_numbers(where_ref, group):
    xl, z, c, xh, y = (where_ref[i] for i in range(5))
    sign = 1 - 2 * c
    numbers = [[], []]
    for d in group:
        for side in range(2):
            if d in (0, 4):
                cores = (c,) if side == 0 else (1 - c,)
                chip = lax.rem(z + d, Z)
            else:
                cores = (c, 1 - c) if side == 0 else (1 - c, c)
                chip = lax.rem(z + Z + sign * (d if side == 0 else -d), Z)
            for core in cores:
                start = ((xl * Z + chip) * C + core) * ROWS + (xh * Y + y) * SHARE
                numbers[side].append(lax.broadcasted_iota(jnp.int32, (SHARE, 1), 0) + start)
    return jnp.concatenate(numbers[0] + numbers[1], axis=0).astype(f32)


def tile_kernel(group, kind, gives, where_ref, *refs):
    refs = list(refs)
    take = lambda count: [refs.pop(0) for _ in range(count)]
    if kind == "first":
        parts = take(4)
    else:
        images_ref, labels_ref, held = take(3)
    texts = take(2 * len(group))
    if kind == "first":
        images_ref, labels_ref = take(2)
        arrange(where_ref, parts, images_ref, labels_ref)
    image_outs = take(4 if kind == "last" else 1)
    term_refs = take(len(group) + gives)
    text_ref, weight_ref = refs
    at = 0
    for side in range(2):
        for i in range(len(group)):
            piece = texts[2 * i + side]
            text_ref[at : at + piece.shape[0], :] = piece[...]
            at += piece.shape[0]
    numbers = text_numbers(where_ref, group)
    text = text_ref[...]
    for a in range(0, 1024, 256):
        cut = slice(a, a + 256)
        logits = (
            lax.dot_general(text, images_ref[cut, :], (((1,), (1,)), ((), ())), preferred_element_type=f32)
            + logit_bias
        )
        positive = (labels_ref[0:1, cut] == numbers).astype(f32)
        weight_ref[:, cut] = (jax.nn.sigmoid(logits) - positive).astype(low)
    total = lax.dot_general(weight_ref[...], text, (((0,), (0,)), ((), ())), preferred_element_type=f32)
    if kind != "first":
        total = total + held[...]
    if kind == "last":
        for k, ref in enumerate(image_outs):
            ref[...] = total[k * 256 : (k + 1) * 256].astype(low)
    else:
        image_outs[0][...] = total
    term = jnp.dot(weight_ref[...], images_ref[...], preferred_element_type=f32)
    at = 0
    for ref in term_refs:
        ref[...] = term[at : at + ref.shape[0]].astype(ref.dtype)
        at += ref.shape[0]


def tile(where, args, group, kind, sizes, give_sizes):
    width = args[0].shape[1]
    n = 2 * sum(sizes)
    shape = jax.ShapeDtypeStruct
    outs = []
    if kind == "first":
        outs += [shape((1024, width), low), shape((8, 1024), f32)]
    if kind == "last":
        outs += [shape((256, width), low)] * 4
    else:
        outs += [shape((1024, width), f32)]
    outs += [shape((size, width), f32) for size in sizes]
    outs += [shape((size, width), low) for size in give_sizes]
    return pl.pallas_call(
        functools.partial(tile_kernel, group, kind, len(give_sizes)),
        out_shape=tuple(outs),
        in_specs=[pl.BlockSpec(memory_space=pltpu.SMEM)] + [VMEM] * len(args),
        out_specs=(VMEM,) * len(outs),
        scratch_shapes=[pltpu.VMEM((n, width), low), pltpu.VMEM((n, 1024), low)],
        compiler_params=pltpu.CompilerParams(vmem_limit_bytes=28 * MIB),
        cost_estimate=pl.CostEstimate(
            flops=18 * 1024 * n * width, bytes_accessed=4 << 20, transcendentals=1024 * n
        ),
    )(where, *args)


def after(value, *others):
    return lax.optimization_barrier((value, *others))[0]


def on_device(images, texts, labels):
    where = jnp.stack(place()).astype(jnp.int32)
    label_rows = labels.reshape(4, 128)
    text_own = own_text(where, texts)
    text_other = to_core(text_own)
    image_near = prep(where, images, label_rows, False)
    chunk = jnp.concatenate([text_own, text_other], axis=0)
    arrived_2 = to_z(chunk, -2)
    image_near = after(image_near, chunk)
    image_right = to_x(image_near, -1)
    image_left = to_x(image_near, 1)
    arrived_1 = to_z(chunk, -1)
    swapped_1 = to_core(arrived_1)
    image_far = prep(where, images, label_rows, True)
    arrived_2 = after(arrived_2, swapped_1, image_far)
    arrived_3 = to_z(arrived_2, -1)
    arrived_4 = to_z(arrived_2[:SHARE], -2)
    swapped_2 = to_core(after(arrived_2, image_right, image_left))

    args = (image_near, after(image_right, arrived_2), image_far, image_left)
    args += (text_own, text_other, arrived_1, swapped_1)
    image_rows, label_row, held, own_keep, keep_1, own_give, give_1 = tile(
        where, args, (0, 1), "first", (SHARE, 2 * SHARE), (SHARE, 2 * SHARE)
    )
    args = (image_rows, label_row, held, arrived_2, swapped_2)
    held, keep_2, give_2 = tile(where, args, (2,), "middle", (2 * SHARE,), (2 * SHARE,))
    arrived_3 = after(arrived_3, held)
    arrived_4 = after(arrived_4, held)
    swapped_4 = to_core(arrived_4)
    swapped_3 = to_core(arrived_3)
    term_1 = (keep_1 + to_core(give_1).astype(f32)).astype(low)

    term_2 = keep_2 + to_core(give_2).astype(f32)
    held, term_1 = lax.optimization_barrier((held, term_1))
    args = (image_rows, label_row, held, arrived_3, swapped_3, arrived_4, swapped_4)
    sizes = (2 * SHARE, SHARE)
    image_2, image_1, image_3, image_0, keep_3, keep_4, give_3, give_4 = tile(
        where, args, (3, 4), "last", sizes, sizes
    )
    from_1 = to_z(term_1, 1)
    back_3, back_4 = to_core(give_3), to_core(give_4)
    back_3, back_4 = after(back_3, from_1), after(back_4, from_1)
    from_3 = to_z((keep_3 + back_3.astype(f32)).astype(low), 1).astype(f32)
    from_4 = to_z((keep_4 + back_4.astype(f32)).astype(low), 2).astype(f32)
    upper = term_2[:SHARE] + from_3[:SHARE] + from_4
    lower = term_2[SHARE:] + from_3[SHARE:]
    term_2 = jnp.concatenate([upper, lower], axis=0).astype(low)
    parts = from_1.astype(f32) + to_z(term_2, 2).astype(f32)

    state = (image_0, image_1, image_2, image_3)
    arrived = [first_stage(state[d], d) for d in (2, 1, 3)]
    arrived = list(lax.optimization_barrier((*arrived, term_2))[:3])
    image_sum = state[0].astype(f32)
    for value in arrived:
        image_sum = image_sum + value.astype(f32)
    image_out = image_sum[:SHARE]
    for d in (2, 1, 3):
        piece = image_sum[d * SHARE : (d + 1) * SHARE].astype(low)
        image_out = image_out + second_stage(piece, d).astype(f32)

    give = (parts[SHARE:] + own_give.astype(f32)).astype(low)
    text_out = parts[:SHARE] + own_keep + to_core(give).astype(f32)
    return image_out, text_out


def solution(mesh):
    placed = (P("block", None), P("block", None), P("block"))
    return jax.shard_map(
        on_device,
        mesh=mesh,
        in_specs=placed,
        out_specs=(P(("block", "lane"), None), P(("block", "lane"), None)),
        check_vma=False,
    )
```

```python
import functools

import jax
import jax.numpy as jnp
from jax import lax
from jax.experimental import pallas as pl
from jax.experimental.pallas import tpu as pltpu
from jax.sharding import PartitionSpec as P

logit_bias = -6.0
Z, C, X, Y = 8, 2, 4, 4
AXES = ("block", "lane")
ROWS = 512
SHARE = 64
low = jnp.bfloat16
f32 = jnp.float32
MIB = 1 << 20
ORDER = (2, 1, 3, 0)
VMEM = pl.BlockSpec(memory_space=pltpu.VMEM)
HBM = pl.BlockSpec(memory_space=pltpu.HBM)


def flat(x, y, z, c):
    return (((x % 2) * Z + z) * C + c) * (X // 2 * Y) + (x // 2) * Y + y


def send(value, step):
    pairs = []
    for x in range(X):
        for y in range(Y):
            for z in range(Z):
                for c in range(C):
                    dx, dy, dz, dc = step(c)
                    to = flat((x + dx) % X, (y + dy) % Y, (z + dz) % Z, (c + dc) % C)
                    pairs.append((flat(x, y, z, c), to))
    return lax.ppermute(value, AXES, pairs)


def to_core(value):
    return send(value, lambda c: (0, 0, 0, 1))


def to_x(value, d):
    return send(value, lambda c: (d, 0, 0, 0))


def to_z(value, d):
    return send(value, lambda c: (0, 0, -d if c else d, 0))


def first_stage(value, d):
    return send(value, lambda c: (0, d, 0, 0) if c else (d, 0, 0, 0))


def second_stage(value, d):
    return send(value, lambda c: (d, 0, 0, 0) if c else (0, d, 0, 0))


def place():
    block = lax.axis_index("block")
    lane = lax.axis_index("lane")
    return block // 16, block // 2 % 8, block % 2, lane // 4, lane % 4


def prep_kernel(far, images_ref, labels_ref, image_out, held, sems):
    xh, y = place()[3:]
    half = 1 - xh if far else xh
    copies = []
    for i in range(Y):
        row = pl.multiple_of((half * Y + lax.rem(y + i, Y)) * SHARE, SHARE)
        copy = pltpu.make_async_copy(images_ref.at[pl.ds(row, SHARE)], held.at[i], sems.at[i])
        copy.start()
        copies.append(copy)
    labels = jnp.concatenate([labels_ref[pl.ds(2 * half, 1), :], labels_ref[pl.ds(2 * half + 1, 1), :]], axis=1)
    labels = jnp.broadcast_to(labels, (16, 256))
    labels = pltpu.roll(labels, lax.rem(Y - y, Y) * SHARE, 1)
    row = lax.broadcasted_iota(jnp.int32, (16, 256), 0)
    digits = jnp.where(row == 0, labels >> 7, jnp.where(row == 1, labels & 127, 0))
    image_out[256:272, :256] = digits.astype(f32).astype(low)
    image_out[256:272, 256:] = jnp.zeros((16, image_out.shape[1] - 256), low)
    for i in range(Y):
        copies[i].wait()
        image_out[i * SHARE : (i + 1) * SHARE, :] = held[i].astype(low)


def prep(images, labels, far):
    width = images.shape[1]
    return pl.pallas_call(
        functools.partial(prep_kernel, far),
        out_shape=jax.ShapeDtypeStruct((272, width), low),
        in_specs=[HBM, VMEM],
        out_specs=VMEM,
        scratch_shapes=[pltpu.VMEM((Y, SHARE, width), f32), pltpu.SemaphoreType.DMA((Y,))],
        compiler_params=pltpu.CompilerParams(vmem_limit_bytes=52 * MIB),
        cost_estimate=pl.CostEstimate(flops=0, bytes_accessed=3 << 20, transcendentals=0),
    )(images, labels)


def text_kernel(texts_ref, text_out, held, sem):
    row = pl.multiple_of(lax.axis_index("lane") * SHARE, SHARE)
    copy = pltpu.make_async_copy(texts_ref.at[pl.ds(row, SHARE)], held, sem)
    copy.start()
    copy.wait()
    text_out[...] = held[...].astype(low)


def own_text(texts):
    width = texts.shape[1]
    return pl.pallas_call(
        text_kernel,
        out_shape=jax.ShapeDtypeStruct((SHARE, width), low),
        in_specs=[HBM],
        out_specs=VMEM,
        scratch_shapes=[pltpu.VMEM((SHARE, width), f32), pltpu.SemaphoreType.DMA],
        compiler_params=pltpu.CompilerParams(vmem_limit_bytes=52 * MIB),
        cost_estimate=pl.CostEstimate(flops=0, bytes_accessed=1 << 19, transcendentals=0),
    )(texts)


def arrange(parts, images_ref, labels_ref):
    labels = []
    for part in parts:
        digits = part[256:272, :256].astype(f32)
        labels.append(digits[0:1] * 128.0 + digits[1:2])
    core = place()[2]

    @pl.when(core == 0)
    def _():
        for k, d in enumerate(ORDER):
            images_ref[k * 256 : (k + 1) * 256, :] = parts[d][:256, :]
            labels_ref[:, k * 256 : (k + 1) * 256] = jnp.broadcast_to(labels[d], (8, 256))

    @pl.when(core == 1)
    def _():
        for k, d in enumerate(ORDER):
            cut = slice(d * SHARE, (d + 1) * SHARE)
            for a in range(4):
                start = k * 256 + a * SHARE
                images_ref[start : start + SHARE, :] = parts[a][cut, :]
            row = jnp.concatenate([labels[a][:, cut] for a in range(4)], axis=1)
            labels_ref[:, k * 256 : (k + 1) * 256] = jnp.broadcast_to(row, (8, 256))


def text_numbers(group):
    xl, z, c, xh, y = place()
    sign = 1 - 2 * c
    numbers = [[], []]
    for d in group:
        for side in range(2):
            if d in (0, 4):
                cores = (c,) if side == 0 else (1 - c,)
                chip = lax.rem(z + d, Z)
            else:
                cores = (c, 1 - c) if side == 0 else (1 - c, c)
                chip = lax.rem(z + Z + sign * (d if side == 0 else -d), Z)
            for core in cores:
                start = ((xl * Z + chip) * C + core) * ROWS + (xh * Y + y) * SHARE
                numbers[side].append(lax.broadcasted_iota(jnp.int32, (SHARE, 1), 0) + start)
    return jnp.concatenate(numbers[0] + numbers[1], axis=0).astype(f32)


def tile_kernel(group, kind, gives, *refs):
    refs = list(refs)
    take = lambda count: [refs.pop(0) for _ in range(count)]
    if kind == "first":
        parts = take(4)
    else:
        images_ref, labels_ref, held = take(3)
    texts = take(2 * len(group))
    if kind == "first":
        images_ref, labels_ref = take(2)
        arrange(parts, images_ref, labels_ref)
    image_outs = take(4 if kind == "last" else 1)
    term_refs = take(len(group) + gives)
    text_ref, weight_ref = refs
    at = 0
    for side in range(2):
        for i in range(len(group)):
            piece = texts[2 * i + side]
            text_ref[at : at + piece.shape[0], :] = piece[...]
            at += piece.shape[0]
    numbers = text_numbers(group)
    text = text_ref[...]
    for a in range(0, 1024, 256):
        cut = slice(a, a + 256)
        logits = (
            lax.dot_general(text, images_ref[cut, :], (((1,), (1,)), ((), ())), preferred_element_type=f32)
            + logit_bias
        )
        positive = (labels_ref[0:1, cut] == numbers).astype(f32)
        weight_ref[:, cut] = (jax.nn.sigmoid(logits) - positive).astype(low)
    total = lax.dot_general(weight_ref[...], text, (((0,), (0,)), ((), ())), preferred_element_type=f32)
    if kind != "first":
        total = total + held[...]
    if kind == "last":
        for k, ref in enumerate(image_outs):
            ref[...] = total[k * 256 : (k + 1) * 256].astype(low)
    else:
        image_outs[0][...] = total
    term = jnp.dot(weight_ref[...], images_ref[...], preferred_element_type=f32)
    at = 0
    for ref in term_refs:
        ref[...] = term[at : at + ref.shape[0]].astype(ref.dtype)
        at += ref.shape[0]


def tile(args, group, kind, sizes, give_sizes):
    width = args[0].shape[1]
    n = 2 * sum(sizes)
    shape = jax.ShapeDtypeStruct
    outs = []
    if kind == "first":
        outs += [shape((1024, width), low), shape((8, 1024), f32)]
    if kind == "last":
        outs += [shape((256, width), low)] * 4
    else:
        outs += [shape((1024, width), f32)]
    outs += [shape((size, width), f32) for size in sizes]
    outs += [shape((size, width), low) for size in give_sizes]
    return pl.pallas_call(
        functools.partial(tile_kernel, group, kind, len(give_sizes)),
        out_shape=tuple(outs),
        in_specs=[VMEM] * len(args),
        out_specs=(VMEM,) * len(outs),
        scratch_shapes=[pltpu.VMEM((n, width), low), pltpu.VMEM((n, 1024), low)],
        compiler_params=pltpu.CompilerParams(vmem_limit_bytes=28 * MIB),
        cost_estimate=pl.CostEstimate(
            flops=18 * 1024 * n * width, bytes_accessed=4 << 20, transcendentals=1024 * n
        ),
    )(*args)


def after(value, *others):
    return lax.optimization_barrier((value, *others))[0]


def on_device(images, texts, labels):
    label_rows = labels.reshape(4, 128)
    text_own = own_text(texts)
    text_other = to_core(text_own)
    image_near = prep(images, label_rows, False)
    chunk = jnp.concatenate([text_own, text_other], axis=0)
    arrived_2 = to_z(chunk, -2)
    image_near = after(image_near, chunk)
    image_right = to_x(image_near, -1)
    image_left = to_x(image_near, 1)
    arrived_1 = to_z(chunk, -1)
    swapped_1 = to_core(arrived_1)
    image_far = prep(images, label_rows, True)
    arrived_2 = after(arrived_2, swapped_1, image_far)
    arrived_3 = to_z(arrived_2, -1)
    arrived_4 = to_z(arrived_2[:SHARE], -2)
    swapped_2 = to_core(after(arrived_2, image_right, image_left))

    args = (image_near, after(image_right, arrived_2), image_far, image_left)
    args += (arrived_1, swapped_1)
    image_rows, label_row, held, keep_1, give_1 = tile(args, (1,), "first", (2 * SHARE,), (2 * SHARE,))
    args = (image_rows, label_row, held, arrived_2, swapped_2)
    held, keep_2, give_2 = tile(args, (2,), "middle", (2 * SHARE,), (2 * SHARE,))
    arrived_3 = after(arrived_3, held)
    arrived_4 = after(arrived_4, held)
    swapped_4 = to_core(arrived_4)
    swapped_3 = to_core(arrived_3)
    term_1 = (keep_1 + to_core(give_1).astype(f32)).astype(low)

    term_2 = keep_2 + to_core(give_2).astype(f32)
    held, term_1 = lax.optimization_barrier((held, term_1))
    args = (image_rows, label_row, held)
    args += (text_own, text_other, arrived_3, swapped_3, arrived_4, swapped_4)
    sizes = (SHARE, 2 * SHARE, SHARE)
    image_2, image_1, image_3, image_0, own_keep, keep_3, keep_4, own_give, give_3, give_4 = tile(
        args, (0, 3, 4), "last", sizes, sizes
    )
    from_1 = to_z(term_1, 1)
    back_3, back_4 = to_core(give_3), to_core(give_4)
    back_3, back_4 = after(back_3, from_1), after(back_4, from_1)
    from_3 = to_z((keep_3 + back_3.astype(f32)).astype(low), 1).astype(f32)
    from_4 = to_z((keep_4 + back_4.astype(f32)).astype(low), 2).astype(f32)
    upper = term_2[:SHARE] + from_3[:SHARE] + from_4
    lower = term_2[SHARE:] + from_3[SHARE:]
    term_2 = jnp.concatenate([upper, lower], axis=0).astype(low)
    parts = from_1.astype(f32) + to_z(term_2, 2).astype(f32)

    state = (image_0, image_1, image_2, image_3)
    arrived = [first_stage(state[d], d) for d in (2, 1, 3)]
    arrived = list(lax.optimization_barrier((*arrived, term_2))[:3])
    image_sum = state[0].astype(f32)
    for value in arrived:
        image_sum = image_sum + value.astype(f32)
    image_out = image_sum[:SHARE]
    for d in (2, 1, 3):
        piece = image_sum[d * SHARE : (d + 1) * SHARE].astype(low)
        image_out = image_out + second_stage(piece, d).astype(f32)

    give = (parts[SHARE:] + own_give.astype(f32)).astype(low)
    text_out = parts[:SHARE] + own_keep + to_core(give).astype(f32)
    return image_out, text_out


def solution(mesh):
    placed = (P("block", None), P("block", None), P("block"))
    return jax.shard_map(
        on_device,
        mesh=mesh,
        in_specs=placed,
        out_specs=(P(("block", "lane"), None), P(("block", "lane"), None)),
        check_vma=False,
    )
```

```python
import functools

import jax
import jax.numpy as jnp
from jax import lax
from jax.experimental import pallas as pl
from jax.experimental.pallas import tpu as pltpu
from jax.sharding import PartitionSpec as P

logit_bias = -6.0
Z, C, X, Y = 8, 2, 4, 4
AXES = ("block", "lane")
ROWS = 512
SHARE = 64
low = jnp.bfloat16
f32 = jnp.float32
MIB = 1 << 20
ORDER = (1, 3, 2, 0)
VMEM = pl.BlockSpec(memory_space=pltpu.VMEM)
HBM = pl.BlockSpec(memory_space=pltpu.HBM)


def flat(x, y, z, c):
    return (((x % 2) * Z + z) * C + c) * (X // 2 * Y) + (x // 2) * Y + y


def send(value, step):
    pairs = []
    for x in range(X):
        for y in range(Y):
            for z in range(Z):
                for c in range(C):
                    dx, dy, dz, dc = step(c)
                    to = flat((x + dx) % X, (y + dy) % Y, (z + dz) % Z, (c + dc) % C)
                    pairs.append((flat(x, y, z, c), to))
    return lax.ppermute(value, AXES, pairs)


def to_core(value):
    return send(value, lambda c: (0, 0, 0, 1))


def to_x(value, d):
    return send(value, lambda c: (d, 0, 0, 0))


def to_z(value, d):
    return send(value, lambda c: (0, 0, -d if c else d, 0))


def first_stage(value, d):
    return send(value, lambda c: (0, d, 0, 0) if c else (d, 0, 0, 0))


def second_stage(value, d):
    return send(value, lambda c: (d, 0, 0, 0) if c else (0, d, 0, 0))


def place():
    block = lax.axis_index("block")
    lane = lax.axis_index("lane")
    return block // 16, block // 2 % 8, block % 2, lane // 4, lane % 4


def prep_kernel(far, images_ref, labels_ref, image_out, held, sems):
    xh, y = place()[3:]
    half = 1 - xh if far else xh
    copies = []
    for i in range(Y):
        row = pl.multiple_of((half * Y + lax.rem(y + i, Y)) * SHARE, SHARE)
        copy = pltpu.make_async_copy(images_ref.at[pl.ds(row, SHARE)], held.at[i], sems.at[i])
        copy.start()
        copies.append(copy)
    labels = jnp.concatenate([labels_ref[pl.ds(2 * half, 1), :], labels_ref[pl.ds(2 * half + 1, 1), :]], axis=1)
    labels = jnp.broadcast_to(labels, (16, 256))
    labels = pltpu.roll(labels, lax.rem(Y - y, Y) * SHARE, 1)
    row = lax.broadcasted_iota(jnp.int32, (16, 256), 0)
    digits = jnp.where(row == 0, labels >> 7, jnp.where(row == 1, labels & 127, 0))
    image_out[256:272, :256] = digits.astype(f32).astype(low)
    image_out[256:272, 256:] = jnp.zeros((16, image_out.shape[1] - 256), low)
    for i in range(Y):
        copies[i].wait()
        image_out[i * SHARE : (i + 1) * SHARE, :] = held[i].astype(low)


def prep(images, labels, far):
    width = images.shape[1]
    return pl.pallas_call(
        functools.partial(prep_kernel, far),
        out_shape=jax.ShapeDtypeStruct((272, width), low),
        in_specs=[HBM, VMEM],
        out_specs=VMEM,
        scratch_shapes=[pltpu.VMEM((Y, SHARE, width), f32), pltpu.SemaphoreType.DMA((Y,))],
        compiler_params=pltpu.CompilerParams(vmem_limit_bytes=52 * MIB),
        cost_estimate=pl.CostEstimate(flops=0, bytes_accessed=3 << 20, transcendentals=0),
    )(images, labels)


def text_kernel(texts_ref, text_out, held, sem):
    row = pl.multiple_of(lax.axis_index("lane") * SHARE, SHARE)
    copy = pltpu.make_async_copy(texts_ref.at[pl.ds(row, SHARE)], held, sem)
    copy.start()
    copy.wait()
    text_out[...] = held[...].astype(low)


def own_text(texts):
    width = texts.shape[1]
    return pl.pallas_call(
        text_kernel,
        out_shape=jax.ShapeDtypeStruct((SHARE, width), low),
        in_specs=[HBM],
        out_specs=VMEM,
        scratch_shapes=[pltpu.VMEM((SHARE, width), f32), pltpu.SemaphoreType.DMA],
        compiler_params=pltpu.CompilerParams(vmem_limit_bytes=52 * MIB),
        cost_estimate=pl.CostEstimate(flops=0, bytes_accessed=1 << 19, transcendentals=0),
    )(texts)


def arrange(parts, images_ref, labels_ref):
    labels = []
    for part in parts:
        digits = part[256:272, :256].astype(f32)
        labels.append(digits[0:1] * 128.0 + digits[1:2])
    core = place()[2]

    @pl.when(core == 0)
    def _():
        for k, d in enumerate(ORDER):
            images_ref[k * 256 : (k + 1) * 256, :] = parts[d][:256, :]
            labels_ref[:, k * 256 : (k + 1) * 256] = jnp.broadcast_to(labels[d], (8, 256))

    @pl.when(core == 1)
    def _():
        for k, d in enumerate(ORDER):
            cut = slice(d * SHARE, (d + 1) * SHARE)
            for a in range(4):
                start = k * 256 + a * SHARE
                images_ref[start : start + SHARE, :] = parts[a][cut, :]
            row = jnp.concatenate([labels[a][:, cut] for a in range(4)], axis=1)
            labels_ref[:, k * 256 : (k + 1) * 256] = jnp.broadcast_to(row, (8, 256))


def text_numbers(group):
    xl, z, c, xh, y = place()
    sign = 1 - 2 * c
    numbers = [[], []]
    for d in group:
        for side in range(2):
            if d in (0, 4):
                cores = (c,) if side == 0 else (1 - c,)
                chip = lax.rem(z + d, Z)
            else:
                cores = (c, 1 - c) if side == 0 else (1 - c, c)
                chip = lax.rem(z + Z + sign * (d if side == 0 else -d), Z)
            for core in cores:
                start = ((xl * Z + chip) * C + core) * ROWS + (xh * Y + y) * SHARE
                numbers[side].append(lax.broadcasted_iota(jnp.int32, (SHARE, 1), 0) + start)
    return jnp.concatenate(numbers[0] + numbers[1], axis=0).astype(f32)


def tile_kernel(group, kind, gives, *refs):
    refs = list(refs)
    take = lambda count: [refs.pop(0) for _ in range(count)]
    if kind == "first":
        parts = take(4)
    else:
        images_ref, labels_ref, held = take(3)
    texts = take(2 * len(group))
    if kind == "first":
        images_ref, labels_ref = take(2)
        arrange(parts, images_ref, labels_ref)
    image_outs = take(4 if kind == "last" else 1)
    term_refs = take(len(group) + gives)
    text_ref, weight_ref = refs
    at = 0
    for side in range(2):
        for i in range(len(group)):
            piece = texts[2 * i + side]
            text_ref[at : at + piece.shape[0], :] = piece[...]
            at += piece.shape[0]
    numbers = text_numbers(group)
    text = text_ref[...]
    for a in range(0, 1024, 256):
        cut = slice(a, a + 256)
        logits = (
            lax.dot_general(text, images_ref[cut, :], (((1,), (1,)), ((), ())), preferred_element_type=f32)
            + logit_bias
        )
        positive = (labels_ref[0:1, cut] == numbers).astype(f32)
        weight_ref[:, cut] = (jax.nn.sigmoid(logits) - positive).astype(low)
    total = lax.dot_general(weight_ref[...], text, (((0,), (0,)), ((), ())), preferred_element_type=f32)
    if kind != "first":
        total = total + held[...]
    if kind == "last":
        for k, ref in enumerate(image_outs):
            ref[...] = total[k * 256 : (k + 1) * 256].astype(low)
    else:
        image_outs[0][...] = total
    term = jnp.dot(weight_ref[...], images_ref[...], preferred_element_type=f32)
    at = 0
    for ref in term_refs:
        ref[...] = term[at : at + ref.shape[0]].astype(ref.dtype)
        at += ref.shape[0]


def tile(args, group, kind, sizes, give_sizes):
    width = args[0].shape[1]
    n = 2 * sum(sizes)
    shape = jax.ShapeDtypeStruct
    outs = []
    if kind == "first":
        outs += [shape((1024, width), low), shape((8, 1024), f32)]
    if kind == "last":
        outs += [shape((256, width), low)] * 4
    else:
        outs += [shape((1024, width), f32)]
    outs += [shape((size, width), f32) for size in sizes]
    outs += [shape((size, width), low) for size in give_sizes]
    return pl.pallas_call(
        functools.partial(tile_kernel, group, kind, len(give_sizes)),
        out_shape=tuple(outs),
        in_specs=[VMEM] * len(args),
        out_specs=(VMEM,) * len(outs),
        scratch_shapes=[pltpu.VMEM((n, width), low), pltpu.VMEM((n, 1024), low)],
        compiler_params=pltpu.CompilerParams(vmem_limit_bytes=28 * MIB),
        cost_estimate=pl.CostEstimate(
            flops=18 * 1024 * n * width, bytes_accessed=4 << 20, transcendentals=1024 * n
        ),
    )(*args)


def after(value, *others):
    return lax.optimization_barrier((value, *others))[0]


def on_device(images, texts, labels):
    label_rows = labels.reshape(4, 128)
    text_own = own_text(texts)
    text_other = to_core(text_own)
    image_near = prep(images, label_rows, False)
    chunk = jnp.concatenate([text_own, text_other], axis=0)
    arrived_2 = to_z(chunk, -2)
    image_near = after(image_near, chunk)
    image_right = to_x(image_near, -1)
    image_left = to_x(image_near, 1)
    arrived_1 = to_z(chunk, -1)
    swapped_1 = to_core(arrived_1)
    image_far = prep(images, label_rows, True)
    arrived_2 = after(arrived_2, swapped_1, image_far)
    arrived_3 = to_z(arrived_2, -1)
    arrived_4 = to_z(arrived_2[:SHARE], -2)
    swapped_2 = to_core(after(arrived_2, image_right, image_left))

    args = (image_near, after(image_right, arrived_2), image_far, image_left)
    args += (arrived_1, swapped_1)
    image_rows, label_row, held, keep_1, give_1 = tile(args, (1,), "first", (2 * SHARE,), (2 * SHARE,))
    args = (image_rows, label_row, held, arrived_2, swapped_2)
    held, keep_2, give_2 = tile(args, (2,), "middle", (2 * SHARE,), (2 * SHARE,))
    arrived_3 = after(arrived_3, held)
    arrived_4 = after(arrived_4, held)
    swapped_4 = to_core(arrived_4)
    swapped_3 = to_core(arrived_3)
    term_1 = (keep_1 + to_core(give_1).astype(f32)).astype(low)

    term_2 = keep_2 + to_core(give_2).astype(f32)
    held, term_1 = lax.optimization_barrier((held, term_1))
    args = (image_rows, label_row, held)
    args += (text_own, text_other, arrived_3, swapped_3, arrived_4, swapped_4)
    sizes = (SHARE, 2 * SHARE, SHARE)
    image_1, image_3, image_2, image_0, own_keep, keep_3, keep_4, own_give, give_3, give_4 = tile(
        args, (0, 3, 4), "last", sizes, sizes
    )
    from_1 = to_z(term_1, 1)
    back_3, back_4 = to_core(give_3), to_core(give_4)
    back_3, back_4 = after(back_3, from_1), after(back_4, from_1)
    from_3 = to_z((keep_3 + back_3.astype(f32)).astype(low), 1).astype(f32)
    from_4 = to_z((keep_4 + back_4.astype(f32)).astype(low), 2).astype(f32)
    upper = term_2[:SHARE] + from_3[:SHARE] + from_4
    lower = term_2[SHARE:] + from_3[SHARE:]
    term_2 = jnp.concatenate([upper, lower], axis=0).astype(low)
    parts = from_1.astype(f32) + to_z(term_2, 2).astype(f32)

    state = (image_0, image_1, image_2, image_3)
    arrived = [first_stage(state[d], d) for d in (1, 3, 2)]
    arrived = list(lax.optimization_barrier((*arrived, term_2))[:3])
    image_sum = state[0].astype(f32)
    for value in arrived:
        image_sum = image_sum + value.astype(f32)
    image_out = image_sum[:SHARE]
    for d in (2, 1, 3):
        piece = image_sum[d * SHARE : (d + 1) * SHARE].astype(low)
        image_out = image_out + second_stage(piece, d).astype(f32)

    give = (parts[SHARE:] + own_give.astype(f32)).astype(low)
    text_out = parts[:SHARE] + own_keep + to_core(give).astype(f32)
    return image_out, text_out


def solution(mesh):
    placed = (P("block", None), P("block", None), P("block"))
    return jax.shard_map(
        on_device,
        mesh=mesh,
        in_specs=placed,
        out_specs=(P(("block", "lane"), None), P(("block", "lane"), None)),
        check_vma=False,
    )
```
